32 devices in a mesh: src: 4 (over x, core), tgt: 4 (over z), feat: 2 (over y).
Axes of the slice: x: 2, y: 2, z: 4, core: 2. Of those that a mesh axis runs over, the one named last changes fastest.
Arguments:
- activations: bfloat16 [4, 1792, 1280], P('src', None, 'feat'), may hold values from 0 to 12, as said below
- window_ids: int32 [4, 640], replicated, may hold values from 0 to 1279, as said below
- decoders: bfloat16 [4, 4, 640, 2048], P('src', 'tgt', 'feat'), may hold values from -3 to 3
- encoders: bfloat16 [4, 2048, 640], P('tgt', ('src', 'feat')), may hold values from -0.125 to 0.125
Outputs:
- weighted: float32 [4, 4, 640, 640], P('src', 'tgt', 'feat')
The draws below stay inside these ranges and needn't reach their ends.
Inputs may be any that keep to these rules, and one draw needn't show every extreme that they name: `window_ids`: each layer's list names 640 distinct features. activations are zero or positive.
All inputs are finite; a program needn't handle non-finite values.
Results may differ from the reference program's by a relative error of at most 0.0029.
Values may be sent and summed in bfloat16 or wider, within the bound.
A program may use at most 64 MiB of HBM per device.

```python
import jax
import jax.numpy as jnp
from jax import lax

D = 2048
FEATS = 1280
FW = 640
TOKENS = 1792
LAYERS = 4


def draw_activations(key, part):
    chosen_entry_filter, key_tier = jax.random.split(key, 2)
    full_dimensions = (LAYERS, TOKENS, FEATS)
    active_flag = (jax.random.randint(chosen_entry_filter, full_dimensions, 0, 4) == 0).astype(jnp.float32)
    per_depth_results = jnp.exp(jax.random.uniform(key_tier, full_dimensions, jnp.float32, jnp.log(0.5), jnp.log(6.0)))
    return (active_flag * per_depth_results).astype(jnp.bfloat16)


def draw_window_ids(key, part):

    def one_layer(layer_key):
        key_pick, key_order = jax.random.split(layer_key)
        middle_ids = (jax.random.permutation(key_pick, FEATS - 2)[:FW - 2] + 1).astype(jnp.int32)
        listed = jnp.concatenate([jnp.array([0, FEATS - 1], jnp.int32), middle_ids])
        return listed[jax.random.permutation(key_order, FW)]
    return jax.vmap(one_layer)(jax.random.split(jax.random.fold_in(key, 7), LAYERS))


def block_levels(own_key, extent, cuts, least, high):
    def one(axis_at, parts):
        steps = jax.random.uniform(jax.random.fold_in(jax.random.fold_in(own_key, 6), axis_at), (parts,), jnp.float32, least / len(cuts), high / len(cuts))
        return jnp.repeat(jnp.exp(steps), extent[axis_at] // parts).reshape((-1,) + (1,) * (len(extent) - axis_at - 1))

    level = one(*cuts[0])
    for cut in cuts[1:]:
        level = level * one(*cut)
    return level


def centred(own_key, shape, spread, limit, shards=(), held_as=jnp.bfloat16):
    entries = jax.random.normal(own_key, shape, jnp.float32) * spread
    if len(shards) > 0:
        entries = block_levels(own_key, shape, shards, -0.22, 0.18) * entries
    return jnp.clip(entries, min=-limit, max=limit).astype(held_as)


def setup_inputs(seed: int = 0) -> dict:
    streams_of = jax.random.split(jax.random.key(seed), 5)
    activations = draw_activations(jax.random.fold_in(streams_of[4], 71), 0)
    window_ids = draw_window_ids(jax.random.fold_in(streams_of[4], 71), 0)
    decoders = centred(streams_of[2], (LAYERS, LAYERS, FW, D), 0.5, 3.0, ((0, 4), (1, 4), (2, 2)))
    encoders = centred(streams_of[3], (LAYERS, D, FW), D ** -0.5, 0.125, ((0, 4), (1, 8)))
    return dict(activations=activations, window_ids=window_ids, decoders=decoders, encoders=encoders)


def reference(activations, window_ids, decoders, encoders):
    windows = jax.vmap(lambda acts_layer, ids_layer: jnp.take(acts_layer, ids_layer, axis=1))(activations, window_ids)
    windows_wide = windows.astype(jnp.float32)
    encoders_wide = encoders.astype(jnp.float32)
    depth_numbers = jnp.arange(LAYERS).astype(jnp.int32)

    def one_source(source):
        written = lax.dynamic_index_in_dim(decoders, source, 0, keepdims=False).astype(jnp.float32)
        live_mask = (depth_numbers >= source).astype(jnp.float32)
        written = written * live_mask[:, None, None]
        running = jnp.cumsum(written, 0)
        leading_sum = jnp.concatenate([jnp.zeros_like(running[:1]), running[:-1]], 0).astype(jnp.bfloat16)
        virtual = jnp.einsum("tid,tdj->tij", leading_sum.astype(jnp.float32), encoders_wide, precision=lax.Precision.HIGHEST)
        source_window = lax.dynamic_index_in_dim(windows_wide, source, 0, keepdims=False)
        gram = jnp.einsum("ni,tnj->tij", source_window, windows_wide, precision=lax.Precision.HIGHEST) / TOKENS
        return virtual * gram

    return lax.map(one_source, depth_numbers)
```

```python
import functools

import jax
import jax.numpy as jnp
from jax import lax
from jax.experimental import pallas as pl
from jax.experimental.pallas import tpu as pltpu
from jax.sharding import PartitionSpec as P

MESH = pl.DeviceIdType.MESH
NT = (((1,), (1,)), ((), ()))


def each(count, fn, start=0):
    if count - start <= 8:
        for i in range(start, count):
            fn(i)
    else:
        lax.fori_loop(start, count, lambda i, c: (fn(i), c)[1], 0)


def kernel(S, T, F, acts, ids, dec, enc, out, idcol, pt_send, pt_recv, w_own, w_all, e_all,
           ch_recv, ch_send, prefix, p_s, p_r, e_s, e_r, ef_s, ef_r, w_s, w_r, wf_s, wf_r,
           c_s, c_r, l_s):
    src, tgt, feat = lax.axis_index("src"), lax.axis_index("tgt"), lax.axis_index("feat")
    K, wf = dec.shape[1], dec.shape[2]
    tokens, raw = acts.shape[1], acts.shape[2]
    FW = ids.shape[1]
    half = tokens // 2
    rows = enc.shape[1]
    G = S // 2 * F
    parity = lax.rem(src, 2)
    mate = src + 1 - 2 * parity
    group = (src // 2) * F + feat
    chunk = 32 if wf % 32 == 0 else 16
    chunks = wf // chunk

    barrier = pltpu.get_barrier_semaphore()
    plane = src * F + feat

    def greet(i):
        other = lax.rem(plane + i, S * F)
        pl.semaphore_signal(barrier, inc=1, device_id=(other // F, tgt, lax.rem(other, F)),
                            device_id_type=MESH)

    each(S * F, greet, 1)

    @pl.when(tgt > 0)
    def _():
        pl.semaphore_signal(barrier, inc=1, device_id=(src, tgt - 1, feat), device_id_type=MESH)

    @pl.when(tgt < T - 1)
    def _():
        pl.semaphore_signal(barrier, inc=1, device_id=(src, tgt + 1, feat), device_id_type=MESH)

    own_ids = ids[pl.ds(src, 1), :]
    idcol[...] = jnp.transpose(jnp.broadcast_to(own_ids, (128, FW)))

    def picked(f_index, q):
        col = idcol[pl.ds(pl.multiple_of(f_index * wf, 16), wf), :][:, :1] - feat * raw
        one_hot = (col == lax.broadcasted_iota(jnp.int32, (wf, raw), 1)).astype(
            jnp.float32).astype(jnp.bfloat16)
        return lax.dot_general(one_hot, acts[0, q * half:(q + 1) * half, :], NT,
                               preferred_element_type=jnp.float32).astype(jnp.bfloat16)

    def remote(a, b, s, r, where):
        return pltpu.make_async_remote_copy(src_ref=a, dst_ref=b, send_sem=s, recv_sem=r,
                                            device_id=where, device_id_type=MESH)

    def chain_copy(i):
        at = pl.ds(pl.multiple_of(i * chunk, 16), chunk)
        return remote(ch_send.at[at], ch_recv.at[at], c_s.at[i], c_r.at[i],
                      (src, lax.rem(tgt + 1, T), feat))

    def chain(first, last):
        def step(i, carry):
            at = pl.ds(pl.multiple_of(i * chunk, 16), chunk)

            @pl.when(tgt > 0)
            def _():
                chain_copy(i).wait_recv()

            total = ch_recv[at, :].astype(jnp.float32)
            for k in range(K):
                prefix[k, at, :] = total.astype(jnp.bfloat16)
                live = (tgt * K + k >= src).astype(jnp.float32)
                total = total + dec[0, k, at, :].astype(jnp.float32) * live

            @pl.when(tgt < T - 1)
            def _():
                ch_send[at, :] = total.astype(jnp.bfloat16)
                chain_copy(i).start()
            return carry
        lax.fori_loop(first, last, step, 0)

    def e_at(p):
        return e_all.at[:, pl.ds(pl.multiple_of(p * rows, 16), rows), :]

    def e_place(j, par):
        g = lax.rem(group - j + G, G)
        return (2 * (g // F) + par) * F + lax.rem(g, F)

    def e_copy(j):
        g = lax.rem(group + j, G)
        return remote(enc, e_at(plane), e_s.at[j], e_r.at[j],
                      (2 * (g // F) + parity, tgt, lax.rem(g, F)))

    def e_own_forward():
        return remote(enc, e_at(plane), ef_s.at[0], ef_r.at[0], (mate, tgt, feat))

    def e_forward(j):
        place = e_place(j, parity)
        return remote(e_at(place), e_at(place), ef_s.at[j], ef_r.at[j], (mate, tgt, feat))

    def p_copy(q, j):
        return remote(pt_send.at[q, j - 1], pt_recv.at[q, j - 1], p_s.at[q, j - 1],
                      p_r.at[q, j - 1], (src, tgt, lax.rem(feat + j, F)))

    def w_at(q, k, f):
        return w_all.at[q, k, pl.ds(pl.multiple_of(f * wf, 16), wf), :]

    def w_copy(q, k, j):
        g = lax.rem(group + j, G)
        return remote(w_own.at[q], w_at(q, k, feat), w_s.at[q, k, j], w_r.at[k, feat],
                      (2 * (g // F) + q, tgt, lax.rem(g, F)))

    def w_arrival(k, f):
        return remote(w_own.at[0], w_at(parity, k, f), w_s.at[0, k, 0], w_r.at[k, f],
                      (mate, tgt, feat))

    def w_forward(k, f):
        return remote(w_at(parity, k, f), w_at(parity, k, f), wf_s.at[k, f], wf_r.at[k, f],
                      (mate, tgt, feat))

    def w_forward_in(k, f):
        other = w_at(1 - parity, k, f)
        return remote(other, other, wf_s.at[k, f], wf_r.at[k, f], (mate, tgt, feat))

    def if_sends(q, k, j, fn):
        owner = src == tgt * K + k
        if isinstance(j, int) and j > 0:
            pl.when(owner)(fn)
        else:
            pl.when(owner & ((j > 0) | (parity != q)))(fn)

    @pl.when(tgt == 0)
    def _():
        ch_recv[...] = jnp.zeros_like(ch_recv)

    pl.semaphore_wait(barrier, S * F - 1 + (tgt > 0).astype(jnp.int32)
                      + (tgt < T - 1).astype(jnp.int32))

    @pl.when(tgt == 0)
    def _():
        chain(0, chunks)

    for q in range(2):
        for j in range(1, F):
            pt_send[q, j - 1] = picked(lax.rem(feat + j, F), q)
            p_copy(q, j).start()

    each(G, lambda j: e_copy(j).start(), 1)
    e_own_forward().start()
    local = pltpu.make_async_copy(enc, e_at(plane), l_s)
    local.start()
    for q in range(2):
        w_own[q] = picked(feat, q)
    marks = [0, chunks * 4 // 10, chunks * 8 // 10, chunks]

    def chain_part(n):
        @pl.when(tgt > 0)
        def _():
            chain(marks[n], marks[n + 1])

    for q in range(2):
        chain_part(q)
        for j in range(1, F):
            p_copy(q, j).wait_recv()
            w_own[q] = w_own[q] + pt_recv[q, j - 1]
        for k in range(K):
            def send(j):
                if_sends(q, k, j, lambda: w_copy(q, k, j).start())
            each(G, send)

            @pl.when(src == tgt * K + k)
            def _():
                w_all[q, k, pl.ds(pl.multiple_of(feat * wf, 16), wf), :] = w_own[q]

    def pass_on(j):
        e_copy(j).wait_recv()
        e_forward(j).start()

    each(G, pass_on, 1)
    chain_part(2)

    def mine(k, f):
        return (src == tgt * K + k) & (feat == f)

    def mates(k, f):
        return (mate == tgt * K + k) & (feat == f)

    for k in range(K):
        for f in range(F):
            @pl.when(jnp.logical_not(mine(k, f)))
            def _():
                w_arrival(k, f).wait_recv()

            @pl.when(jnp.logical_not(mates(k, f)))
            def _():
                w_forward(k, f).start()

    e_own_in = lambda j: remote(e_at(e_place(j, 1 - parity)), e_at(e_place(j, 1 - parity)),
                                ef_s.at[j], ef_r.at[j], (mate, tgt, feat))
    each(G, lambda j: e_own_in(j).wait_recv())
    local.wait()
    for k in range(K):
        out[0, k] = jnp.dot(prefix[k], e_all[k], preferred_element_type=jnp.float32)

    for k in range(K):
        for f in range(F):
            @pl.when(jnp.logical_not(mine(k, f)))
            def _():
                w_forward_in(k, f).wait_recv()
        gram = lax.dot_general(w_own[0], w_all[0, k], NT, preferred_element_type=jnp.float32)
        gram += lax.dot_general(w_own[1], w_all[1, k], NT, preferred_element_type=jnp.float32)
        out[0, k] = out[0, k] * (gram / tokens)

    @pl.when(tgt < T - 1)
    def _():
        each(chunks, lambda i: chain_copy(i).wait_send())

    for q in range(2):
        for j in range(1, F):
            p_copy(q, j).wait_send()
        for k in range(K):
            def sent(j):
                if_sends(q, k, j, lambda: w_copy(q, k, j).wait_send())
            each(G, sent)
    each(G, lambda j: e_copy(j).wait_send(), 1)
    e_own_forward().wait_send()
    each(G, lambda j: e_forward(j).wait_send(), 1)
    for k in range(K):
        for f in range(F):
            @pl.when(jnp.logical_not(mates(k, f)))
            def _():
                w_forward(k, f).wait_send()


def solution(mesh):
    S, T, F = mesh.shape["src"], mesh.shape["tgt"], mesh.shape["feat"]

    def per_device(activations, window_ids, decoders, encoders):
        _, tokens, raw = activations.shape
        FW = window_ids.shape[1]
        _, K, wf, D = decoders.shape
        G = S // 2 * F
        bf = jnp.bfloat16
        dma = pltpu.SemaphoreType.DMA
        chunks = wf // (32 if wf % 32 == 0 else 16)
        vmem = pl.BlockSpec(memory_space=pltpu.VMEM)
        return pl.pallas_call(
            functools.partial(kernel, S, T, F),
            out_shape=jax.ShapeDtypeStruct((1, K, wf, FW), jnp.float32),
            in_specs=[vmem] * 4,
            out_specs=vmem,
            scratch_shapes=[
                pltpu.VMEM((FW, 128), jnp.int32),
                pltpu.VMEM((2, F - 1, wf, tokens // 2), bf),
                pltpu.VMEM((2, F - 1, wf, tokens // 2), bf),
                pltpu.VMEM((2, wf, tokens // 2), bf),
                pltpu.VMEM((2, K, FW, tokens // 2), bf),
                pltpu.VMEM((K, D, FW), bf),
                pltpu.VMEM((wf, D), bf),
                pltpu.VMEM((wf, D), bf),
                pltpu.VMEM((K, wf, D), bf),
                dma((2, F - 1)), dma((2, F - 1)),
                dma((G,)), dma((G,)), dma((G,)), dma((G,)),
                dma((2, K, G)), dma((K, F)), dma((K, F)), dma((K, F)),
                dma((chunks,)), dma((chunks,)), dma(()),
            ],
            compiler_params=pltpu.CompilerParams(
                collective_id=0, has_side_effects=True, vmem_limit_bytes=56 * 2**20),
        )(activations, window_ids, decoders, encoders)

    in_specs = (
        P("src", None, "feat"),
        P(),
        P("src", "tgt", "feat", None),
        P("tgt", ("src", "feat"), None),
    )
    return jax.shard_map(
        per_device, mesh=mesh, in_specs=in_specs, out_specs=P("src", "tgt", "feat", None),
        check_vma=False,
    )
```

```python
import functools

import jax
import jax.numpy as jnp
from jax import lax
from jax.experimental import pallas as pl
from jax.experimental.pallas import tpu as pltpu
from jax.sharding import PartitionSpec as P

MESH = pl.DeviceIdType.MESH
NT = (((1,), (1,)), ((), ()))


def each(count, fn, start=0):
    if count - start <= 8:
        for i in range(start, count):
            fn(i)
    else:
        lax.fori_loop(start, count, lambda i, c: (fn(i), c)[1], 0)


def kernel(S, T, F, acts, ids, dec, enc, out, idcol, pt_send, pt_recv, w_own, w_all, e_all,
           ch_recv, ch_send, prefix, p_s, p_r, z_s, z_r, ey_s, ey_r, ex_s, ex_r, ef_s, ef_r, w_s, w_r, wf_s, wf_r,
           c_s, c_r, l_s):
    src, tgt, feat = lax.axis_index("src"), lax.axis_index("tgt"), lax.axis_index("feat")
    K, wf = dec.shape[1], dec.shape[2]
    tokens, raw = acts.shape[1], acts.shape[2]
    FW = ids.shape[1]
    half = tokens // 2
    rows = enc.shape[1]
    G = S // 2 * F
    parity = lax.rem(src, 2)
    mate = src + 1 - 2 * parity
    group = (src // 2) * F + feat
    chunk = 32 if wf % 32 == 0 else 16
    chunks = wf // chunk
    pieces = 2 if wf % 32 == 0 else 1
    part = wf // pieces
    early = lax.rem(tgt, 2)
    late = 1 - early
    H = S // 2
    side = src // 2

    barrier = pltpu.get_barrier_semaphore()
    plane = src * F + feat

    def greet(i):
        other = lax.rem(plane + i, S * F)
        pl.semaphore_signal(barrier, inc=1, device_id=(other // F, tgt, lax.rem(other, F)),
                            device_id_type=MESH)

    each(S * F, greet, 1)

    @pl.when(tgt > 0)
    def _():
        pl.semaphore_signal(barrier, inc=1, device_id=(src, tgt - 1, feat), device_id_type=MESH)

    @pl.when(tgt < T - 1)
    def _():
        pl.semaphore_signal(barrier, inc=1, device_id=(src, tgt + 1, feat), device_id_type=MESH)

    own_ids = ids[pl.ds(src, 1), :]
    idcol[...] = jnp.transpose(jnp.broadcast_to(own_ids, (128, FW)))

    def picked(f_index, r):
        start = pl.multiple_of(f_index * wf + r * part, 16)
        col = idcol[pl.ds(start, part), :][:, :1] - feat * raw
        one_hot = (col == lax.broadcasted_iota(jnp.int32, (part, raw), 1)).astype(
            jnp.float32).astype(jnp.bfloat16)
        some = acts[0, pl.ds(pl.multiple_of(early * half, 16), half), :]
        return lax.dot_general(one_hot, some, NT,
                               preferred_element_type=jnp.float32).astype(jnp.bfloat16)

    def remote(a, b, s, r, where):
        return pltpu.make_async_remote_copy(src_ref=a, dst_ref=b, send_sem=s, recv_sem=r,
                                            device_id=where, device_id_type=MESH)

    def chain_copy(i):
        at = pl.ds(pl.multiple_of(i * chunk, 16), chunk)
        return remote(ch_send.at[at], ch_recv.at[at], c_s.at[i], c_r.at[i],
                      (src, lax.rem(tgt + 1, T), feat))

    def chain(first, last):
        def step(i, carry):
            at = pl.ds(pl.multiple_of(i * chunk, 16), chunk)

            @pl.when(tgt > 0)
            def _():
                chain_copy(i).wait_recv()

            total = ch_recv[at, :].astype(jnp.float32)
            for k in range(K):
                prefix[k, at, :] = total.astype(jnp.bfloat16)
                live = (tgt * K + k >= src).astype(jnp.float32)
                total = total + dec[0, k, at, :].astype(jnp.float32) * live

            @pl.when(tgt < T - 1)
            def _():
                ch_send[at, :] = total.astype(jnp.bfloat16)
                chain_copy(i).start()
            return carry
        lax.fori_loop(first, last, step, 0)

    def e_at(p):
        return e_all.at[:, pl.ds(pl.multiple_of(p * rows, 16), rows), :]

    def place(h, f, par):
        return (2 * h + par) * F + f

    def e_y(j):
        return remote(enc, e_at(plane), ey_s.at[j], ey_r.at[j], (src, tgt, lax.rem(feat + j, F)))

    def e_x(i, j, source=None):
        at = e_at(place(side, lax.rem(feat - j + F, F), parity))
        return remote(enc if source is None else source, at, ex_s.at[i, j], ex_r.at[i, j],
                      (2 * lax.rem(side + i, H) + parity, tgt, feat))

    def e_x_out(i, j):
        if isinstance(j, int) and j == 0:
            return e_x(i, 0)
        return e_x(i, j, e_at(place(side, lax.rem(feat - j + F, F), parity)))

    def e_mate(i, j, par, own=False):
        at = e_at(place(lax.rem(side - i + H, H), lax.rem(feat - j + F, F), par))
        return remote(enc if own else at, at, ef_s.at[i, j], ef_r.at[i, j], (mate, tgt, feat))

    def p_copy(r, j):
        return remote(pt_send.at[r, j - 1], pt_recv.at[r, j - 1], p_s.at[r, j - 1],
                      p_r.at[r, j - 1], (src, tgt, lax.rem(feat + j, F)))

    def z_copy(r, q):
        at = w_own.at[q, pl.ds(r * part, part), :]
        return remote(at, at, z_s.at[r], z_r.at[r], (src, tgt + 1 - 2 * early, feat))

    def w_at(q, k, f):
        return w_all.at[q, k, pl.ds(pl.multiple_of(f * wf, 16), wf), :]

    def w_copy(n, q, k, j):
        g = lax.rem(group + j, G)
        return remote(w_own.at[q], w_at(q, k, feat), w_s.at[n, k, j], w_r.at[k, feat],
                      (2 * (g // F) + q, tgt, lax.rem(g, F)))

    def w_arrival(k, f):
        return remote(w_own.at[0], w_at(parity, k, f), w_s.at[0, k, 0], w_r.at[k, f],
                      (mate, tgt, feat))

    def w_forward(k, f):
        return remote(w_at(parity, k, f), w_at(parity, k, f), wf_s.at[k, f], wf_r.at[k, f],
                      (mate, tgt, feat))

    def w_forward_in(k, f):
        other = w_at(1 - parity, k, f)
        return remote(other, other, wf_s.at[k, f], wf_r.at[k, f], (mate, tgt, feat))

    def if_sends(q, k, j, fn):
        owner = src == tgt * K + k
        if isinstance(j, int) and j > 0:
            pl.when(owner)(fn)
        else:
            pl.when(owner & ((j > 0) | (parity != q)))(fn)

    @pl.when(tgt == 0)
    def _():
        ch_recv[...] = jnp.zeros_like(ch_recv)

    pl.semaphore_wait(barrier, S * F - 1 + (tgt > 0).astype(jnp.int32)
                      + (tgt < T - 1).astype(jnp.int32))

    @pl.when(tgt == 0)
    def _():
        chain(0, chunks)

    for r in range(pieces):
        for j in range(1, F):
            pt_send[r, j - 1] = picked(lax.rem(feat + j, F), r)
            p_copy(r, j).start()

    each(H, lambda i: e_x_out(i, 0).start(), 1)
    e_mate(0, 0, parity, True).start()
    local = pltpu.make_async_copy(enc, e_at(plane), l_s)
    local.start()
    for r in range(pieces):
        w_own[early, r * part:(r + 1) * part] = picked(feat, r)
    marks = [0, chunks * 3 // 10, chunks * 5 // 10, chunks * 8 // 10, chunks]

    def chain_part(n):
        @pl.when(tgt > 0)
        def _():
            chain(marks[n], marks[n + 1])

    def mine(k, f):
        return (src == tgt * K + k) & (feat == f)

    def mates(k, f):
        return (mate == tgt * K + k) & (feat == f)

    def w_send(n, q):
        for k in range(K):
            def send(j):
                if_sends(q, k, j, lambda: w_copy(n, q, k, j).start())
            each(G, send)

            @pl.when(src == tgt * K + k)
            def _():
                w_all[q, k, pl.ds(pl.multiple_of(feat * wf, 16), wf), :] = w_own[q]

    def w_pass():
        for k in range(K):
            for f in range(F):
                @pl.when(jnp.logical_not(mine(k, f)))
                def _():
                    w_arrival(k, f).wait_recv()

                @pl.when(jnp.logical_not(mates(k, f)))
                def _():
                    w_forward(k, f).start()

    chain_part(0)
    for r in range(pieces):
        at = slice(r * part, (r + 1) * part)
        for j in range(1, F):
            p_copy(r, j).wait_recv()
            w_own[early, at] = w_own[early, at] + pt_recv[r, j - 1]
        z_copy(r, early).start()
    w_send(0, early)
    each(F, lambda j: e_y(j).start(), 1)
    chain_part(1)

    def e_turn(j):
        e_y(j).wait_recv()
        each(H, lambda i: e_x_out(i, j).start(), 1)
        e_mate(0, j, parity).start()

    each(F, e_turn, 1)
    chain_part(2)
    for r in range(pieces):
        z_copy(r, late).wait_recv()
    w_send(1, late)
    pl.when(parity == early)(w_pass)

    def e_far(i, j):
        e_x(i, j).wait_recv()
        e_mate(i, j, parity).start()

    each(H, lambda i: each(F, lambda j: e_far(i, j)), 1)
    chain_part(3)
    each(H, lambda i: each(F, lambda j: e_mate(i, j, 1 - parity).wait_recv()))
    local.wait()
    for k in range(K):
        out[0, k] = jnp.dot(prefix[k], e_all[k], preferred_element_type=jnp.float32)
    pl.when(parity == late)(w_pass)

    for k in range(K):
        for f in range(F):
            @pl.when(jnp.logical_not(mine(k, f)))
            def _():
                w_forward_in(k, f).wait_recv()
        gram = lax.dot_general(w_own[0], w_all[0, k], NT, preferred_element_type=jnp.float32)
        gram += lax.dot_general(w_own[1], w_all[1, k], NT, preferred_element_type=jnp.float32)
        out[0, k] = out[0, k] * (gram / tokens)

    @pl.when(tgt < T - 1)
    def _():
        each(chunks, lambda i: chain_copy(i).wait_send())

    for r in range(pieces):
        for j in range(1, F):
            p_copy(r, j).wait_send()
        z_copy(r, early).wait_send()
    for n, q in ((0, early), (1, late)):
        for k in range(K):
            def sent(j):
                if_sends(q, k, j, lambda: w_copy(n, q, k, j).wait_send())
            each(G, sent)
    each(F, lambda j: e_y(j).wait_send(), 1)
    each(H, lambda i: each(F, lambda j: e_x_out(i, j).wait_send()), 1)
    each(H, lambda i: each(F, lambda j: e_mate(i, j, parity).wait_send()))
    for k in range(K):
        for f in range(F):
            @pl.when(jnp.logical_not(mates(k, f)))
            def _():
                w_forward(k, f).wait_send()


def solution(mesh):
    S, T, F = mesh.shape["src"], mesh.shape["tgt"], mesh.shape["feat"]

    def per_device(activations, window_ids, decoders, encoders):
        _, tokens, raw = activations.shape
        FW = window_ids.shape[1]
        _, K, wf, D = decoders.shape
        G = S // 2 * F
        H = S // 2
        pieces = 2 if wf % 32 == 0 else 1
        bf = jnp.bfloat16
        dma = pltpu.SemaphoreType.DMA
        chunks = wf // (32 if wf % 32 == 0 else 16)
        vmem = pl.BlockSpec(memory_space=pltpu.VMEM)
        return pl.pallas_call(
            functools.partial(kernel, S, T, F),
            out_shape=jax.ShapeDtypeStruct((1, K, wf, FW), jnp.float32),
            in_specs=[vmem] * 4,
            out_specs=vmem,
            scratch_shapes=[
                pltpu.VMEM((FW, 128), jnp.int32),
                pltpu.VMEM((pieces, F - 1, wf // pieces, tokens // 2), bf),
                pltpu.VMEM((pieces, F - 1, wf // pieces, tokens // 2), bf),
                pltpu.VMEM((2, wf, tokens // 2), bf),
                pltpu.VMEM((2, K, FW, tokens // 2), bf),
                pltpu.VMEM((K, D, FW), bf),
                pltpu.VMEM((wf, D), bf),
                pltpu.VMEM((wf, D), bf),
                pltpu.VMEM((K, wf, D), bf),
                dma((pieces, F - 1)), dma((pieces, F - 1)), dma((pieces,)), dma((pieces,)),
                dma((F,)), dma((F,)), dma((H, F)), dma((H, F)), dma((H, F)), dma((H, F)),
                dma((2, K, G)), dma((K, F)), dma((K, F)), dma((K, F)),
                dma((chunks,)), dma((chunks,)), dma(()),
            ],
            compiler_params=pltpu.CompilerParams(
                collective_id=0, has_side_effects=True, vmem_limit_bytes=56 * 2**20),
        )(activations, window_ids, decoders, encoders)

    in_specs = (
        P("src", None, "feat"),
        P(),
        P("src", "tgt", "feat", None),
        P("tgt", ("src", "feat"), None),
    )
    return jax.shard_map(
        per_device, mesh=mesh, in_specs=in_specs, out_specs=P("src", "tgt", "feat", None),
        check_vma=False,
    )
```

```python
import functools

import jax
import jax.numpy as jnp
from jax import lax
from jax.experimental import pallas as pl
from jax.experimental.pallas import tpu as pltpu
from jax.sharding import PartitionSpec as P

MESH = pl.DeviceIdType.MESH
NT = (((1,), (1,)), ((), ()))


def each(count, fn, start=0):
    if count - start <= 8:
        for i in range(start, count):
            fn(i)
    else:
        lax.fori_loop(start, count, lambda i, c: (fn(i), c)[1], 0)


def kernel(S, T, F, acts, ids, dec, enc, out, idcol, pt_send, pt_recv, w_own, w_all, e_all,
           ch_recv, ch_send, prefix, p_s, p_r, z_s, z_r, ey_s, ey_r, ex_s, ex_r, ef_s, ef_r, w_s, w_r, wf_s, wf_r,
           c_s, c_r, l_s):
    src, tgt, feat = lax.axis_index("src"), lax.axis_index("tgt"), lax.axis_index("feat")
    K, wf = dec.shape[1], dec.shape[2]
    tokens, raw = acts.shape[1], acts.shape[2]
    FW = ids.shape[1]
    half = tokens // 2
    rows = enc.shape[1]
    G = S // 2 * F
    parity = lax.rem(src, 2)
    mate = src + 1 - 2 * parity
    group = (src // 2) * F + feat
    chunk = 32 if wf % 32 == 0 else 16
    chunks = wf // chunk
    pieces = 2 if wf % 32 == 0 else 1
    part = wf // pieces
    early = lax.rem(tgt, 2)
    has_in = (tgt > 0) & (src < tgt * K)
    has_out = (tgt < T - 1) & (src < (tgt + 1) * K)
    late = 1 - early
    H = S // 2
    side = src // 2

    barrier = pltpu.get_barrier_semaphore()
    plane = src * F + feat

    def greet(i):
        other = lax.rem(plane + i, S * F)
        pl.semaphore_signal(barrier, inc=1, device_id=(other // F, tgt, lax.rem(other, F)),
                            device_id_type=MESH)

    each(S * F, greet, 1)

    @pl.when(tgt > 0)
    def _():
        pl.semaphore_signal(barrier, inc=1, device_id=(src, tgt - 1, feat), device_id_type=MESH)

    @pl.when(tgt < T - 1)
    def _():
        pl.semaphore_signal(barrier, inc=1, device_id=(src, tgt + 1, feat), device_id_type=MESH)

    own_ids = ids[pl.ds(src, 1), :]
    idcol[...] = jnp.transpose(jnp.broadcast_to(own_ids, (128, FW)))

    def picked(f_index, r):
        start = pl.multiple_of(f_index * wf + r * part, 16)
        col = idcol[pl.ds(start, part), :][:, :1] - feat * raw
        one_hot = (col == lax.broadcasted_iota(jnp.int32, (part, raw), 1)).astype(
            jnp.float32).astype(jnp.bfloat16)
        some = acts[0, pl.ds(pl.multiple_of(early * half, 16), half), :]
        return lax.dot_general(one_hot, some, NT,
                               preferred_element_type=jnp.float32).astype(jnp.bfloat16)

    def remote(a, b, s, r, where):
        return pltpu.make_async_remote_copy(src_ref=a, dst_ref=b, send_sem=s, recv_sem=r,
                                            device_id=where, device_id_type=MESH)

    def chain_copy(i):
        at = pl.ds(pl.multiple_of(i * chunk, 16), chunk)
        return remote(ch_send.at[at], ch_recv.at[at], c_s.at[i], c_r.at[i],
                      (src, lax.rem(tgt + 1, T), feat))

    def chain(first, last):
        def step(i, carry):
            at = pl.ds(pl.multiple_of(i * chunk, 16), chunk)

            @pl.when(has_in)
            def _():
                chain_copy(i).wait_recv()

            total = ch_recv[at, :].astype(jnp.float32)
            for k in range(K):
                prefix[k, at, :] = total.astype(jnp.bfloat16)
                live = (tgt * K + k >= src).astype(jnp.float32)
                total = total + dec[0, k, at, :].astype(jnp.float32) * live

            @pl.when(has_out)
            def _():
                ch_send[at, :] = total.astype(jnp.bfloat16)
                chain_copy(i).start()
            return carry
        lax.fori_loop(first, last, step, 0)

    def e_at(p):
        return e_all.at[:, pl.ds(pl.multiple_of(p * rows, 16), rows), :]

    def place(h, f, par):
        return (2 * h + par) * F + f

    def e_y(j):
        return remote(enc, e_at(plane), ey_s.at[j], ey_r.at[j], (src, tgt, lax.rem(feat + j, F)))

    def e_x(i, j, source=None):
        at = e_at(place(side, lax.rem(feat - j + F, F), parity))
        return remote(enc if source is None else source, at, ex_s.at[i, j], ex_r.at[i, j],
                      (2 * lax.rem(side + i, H) + parity, tgt, feat))

    def e_x_out(i, j):
        if isinstance(j, int) and j == 0:
            return e_x(i, 0)
        return e_x(i, j, e_at(place(side, lax.rem(feat - j + F, F), parity)))

    def e_mate(i, j, par, own=False):
        at = e_at(place(lax.rem(side - i + H, H), lax.rem(feat - j + F, F), par))
        return remote(enc if own else at, at, ef_s.at[i, j], ef_r.at[i, j], (mate, tgt, feat))

    def p_copy(r, j):
        return remote(pt_send.at[r, j - 1], pt_recv.at[r, j - 1], p_s.at[r, j - 1],
                      p_r.at[r, j - 1], (src, tgt, lax.rem(feat + j, F)))

    def z_copy(r, q):
        at = w_own.at[q, pl.ds(r * part, part), :]
        return remote(at, at, z_s.at[r], z_r.at[r], (src, tgt + 1 - 2 * early, feat))

    def w_at(q, k, f):
        return w_all.at[q, k, pl.ds(pl.multiple_of(f * wf, 16), wf), :]

    def w_copy(n, q, k, j):
        g = lax.rem(group + j, G)
        return remote(w_own.at[q], w_at(q, k, feat), w_s.at[n, k, j], w_r.at[k, feat],
                      (2 * (g // F) + q, tgt, lax.rem(g, F)))

    def w_arrival(k, f):
        return remote(w_own.at[0], w_at(parity, k, f), w_s.at[0, k, 0], w_r.at[k, f],
                      (mate, tgt, feat))

    def w_forward(k, f):
        return remote(w_at(parity, k, f), w_at(parity, k, f), wf_s.at[k, f], wf_r.at[k, f],
                      (mate, tgt, feat))

    def w_forward_in(k, f):
        other = w_at(1 - parity, k, f)
        return remote(other, other, wf_s.at[k, f], wf_r.at[k, f], (mate, tgt, feat))

    def if_sends(q, k, j, fn):
        owner = src == tgt * K + k
        if isinstance(j, int) and j > 0:
            pl.when(owner)(fn)
        else:
            pl.when(owner & ((j > 0) | (parity != q)))(fn)

    @pl.when(jnp.logical_not(has_in))
    def _():
        ch_recv[...] = jnp.zeros_like(ch_recv)

    pl.semaphore_wait(barrier, S * F - 1 + (tgt > 0).astype(jnp.int32)
                      + (tgt < T - 1).astype(jnp.int32))

    @pl.when(jnp.logical_not(has_in))
    def _():
        chain(0, chunks)

    for r in range(pieces):
        for j in range(1, F):
            pt_send[r, j - 1] = picked(lax.rem(feat + j, F), r)
            p_copy(r, j).start()

    each(H, lambda i: e_x_out(i, 0).start(), 1)
    e_mate(0, 0, parity, True).start()
    local = pltpu.make_async_copy(enc, e_at(plane), l_s)
    local.start()
    for r in range(pieces):
        w_own[early, r * part:(r + 1) * part] = picked(feat, r)
    marks = [0, chunks * 3 // 10, chunks * 5 // 10, chunks * 8 // 10, chunks]

    def chain_part(n):
        @pl.when(has_in)
        def _():
            chain(marks[n], marks[n + 1])

    def mine(k, f):
        return (src == tgt * K + k) & (feat == f)

    def mates(k, f):
        return (mate == tgt * K + k) & (feat == f)

    def w_send(n, q):
        for k in range(K):
            def send(j):
                if_sends(q, k, j, lambda: w_copy(n, q, k, j).start())
            each(G, send)

            @pl.when(src == tgt * K + k)
            def _():
                w_all[q, k, pl.ds(pl.multiple_of(feat * wf, 16), wf), :] = w_own[q]

    def w_pass():
        for k in range(K):
            for f in range(F):
                @pl.when(jnp.logical_not(mine(k, f)))
                def _():
                    w_arrival(k, f).wait_recv()

                @pl.when(jnp.logical_not(mates(k, f)))
                def _():
                    w_forward(k, f).start()

    chain_part(0)
    for r in range(pieces):
        at = slice(r * part, (r + 1) * part)
        for j in range(1, F):
            p_copy(r, j).wait_recv()
            w_own[early, at] = w_own[early, at] + pt_recv[r, j - 1]
        z_copy(r, early).start()
    w_send(0, early)
    each(F, lambda j: e_y(j).start(), 1)
    chain_part(1)

    def e_turn(j):
        e_y(j).wait_recv()
        each(H, lambda i: e_x_out(i, j).start(), 1)
        e_mate(0, j, parity).start()

    each(F, e_turn, 1)
    chain_part(2)
    for r in range(pieces):
        z_copy(r, late).wait_recv()
    w_send(1, late)
    pl.when(parity == early)(w_pass)

    def e_far(i, j):
        e_x(i, j).wait_recv()
        e_mate(i, j, parity).start()

    each(H, lambda i: each(F, lambda j: e_far(i, j)), 1)
    chain_part(3)
    each(H, lambda i: each(F, lambda j: e_mate(i, j, 1 - parity).wait_recv()))
    local.wait()
    for k in range(K):
        out[0, k] = jnp.dot(prefix[k], e_all[k], preferred_element_type=jnp.float32)
    pl.when(parity == late)(w_pass)

    for k in range(K):
        for f in range(F):
            @pl.when(jnp.logical_not(mine(k, f)))
            def _():
                w_forward_in(k, f).wait_recv()
        gram = lax.dot_general(w_own[0], w_all[0, k], NT, preferred_element_type=jnp.float32)
        gram += lax.dot_general(w_own[1], w_all[1, k], NT, preferred_element_type=jnp.float32)
        out[0, k] = out[0, k] * (gram / tokens)

    @pl.when(has_out)
    def _():
        each(chunks, lambda i: chain_copy(i).wait_send())

    for r in range(pieces):
        for j in range(1, F):
            p_copy(r, j).wait_send()
        z_copy(r, early).wait_send()
    for n, q in ((0, early), (1, late)):
        for k in range(K):
            def sent(j):
                if_sends(q, k, j, lambda: w_copy(n, q, k, j).wait_send())
            each(G, sent)
    each(F, lambda j: e_y(j).wait_send(), 1)
    each(H, lambda i: each(F, lambda j: e_x_out(i, j).wait_send()), 1)
    each(H, lambda i: each(F, lambda j: e_mate(i, j, parity).wait_send()))
    for k in range(K):
        for f in range(F):
            @pl.when(jnp.logical_not(mates(k, f)))
            def _():
                w_forward(k, f).wait_send()


def solution(mesh):
    S, T, F = mesh.shape["src"], mesh.shape["tgt"], mesh.shape["feat"]

    def per_device(activations, window_ids, decoders, encoders):
        _, tokens, raw = activations.shape
        FW = window_ids.shape[1]
        _, K, wf, D = decoders.shape
        G = S // 2 * F
        H = S // 2
        pieces = 2 if wf % 32 == 0 else 1
        bf = jnp.bfloat16
        dma = pltpu.SemaphoreType.DMA
        chunks = wf // (32 if wf % 32 == 0 else 16)
        vmem = pl.BlockSpec(memory_space=pltpu.VMEM)
        return pl.pallas_call(
            functools.partial(kernel, S, T, F),
            out_shape=pltpu.VMEM((1, K, wf, FW), jnp.float32),
            in_specs=[vmem] * 4,
            out_specs=vmem,
            scratch_shapes=[
                pltpu.VMEM((FW, 128), jnp.int32),
                pltpu.VMEM((pieces, F - 1, wf // pieces, tokens // 2), bf),
                pltpu.VMEM((pieces, F - 1, wf // pieces, tokens // 2), bf),
                pltpu.VMEM((2, wf, tokens // 2), bf),
                pltpu.VMEM((2, K, FW, tokens // 2), bf),
                pltpu.VMEM((K, D, FW), bf),
                pltpu.VMEM((wf, D), bf),
                pltpu.VMEM((wf, D), bf),
                pltpu.VMEM((K, wf, D), bf),
                dma((pieces, F - 1)), dma((pieces, F - 1)), dma((pieces,)), dma((pieces,)),
                dma((F,)), dma((F,)), dma((H, F)), dma((H, F)), dma((H, F)), dma((H, F)),
                dma((2, K, G)), dma((K, F)), dma((K, F)), dma((K, F)),
                dma((chunks,)), dma((chunks,)), dma(()),
            ],
            compiler_params=pltpu.CompilerParams(
                collective_id=0, has_side_effects=True, vmem_limit_bytes=56 * 2**20),
        )(activations, window_ids, decoders, encoders)

    in_specs = (
        P("src", None, "feat"),
        P(),
        P("src", "tgt", "feat", None),
        P("tgt", ("src", "feat"), None),
    )
    return jax.shard_map(
        per_device, mesh=mesh, in_specs=in_specs, out_specs=P("src", "tgt", "feat", None),
        check_vma=False,
    )
```

```python
import functools

import jax
import jax.numpy as jnp
from jax import lax
from jax.experimental import pallas as pl
from jax.experimental.pallas import tpu as pltpu
from jax.sharding import PartitionSpec as P

MESH = pl.DeviceIdType.MESH
NT = (((1,), (1,)), ((), ()))


def each(count, fn, start=0):
    if count - start <= 8:
        for i in range(start, count):
            fn(i)
    else:
        lax.fori_loop(start, count, lambda i, c: (fn(i), c)[1], 0)


def kernel(S, T, F, acts, ids, dec, enc, out, idcol, pt_send, pt_recv, w_own, w_all, e_all,
           ch_recv, ch_send, prefix, p_s, p_r, z_s, z_r, ey_s, ey_r, ex_s, ex_r, ef_s, ef_r, w_s, w_r, wf_s, wf_r,
           c_s, c_r, l_s):
    src, tgt, feat = lax.axis_index("src"), lax.axis_index("tgt"), lax.axis_index("feat")
    K, wf = dec.shape[1], dec.shape[2]
    tokens, raw = acts.shape[1], acts.shape[2]
    FW = ids.shape[1]
    half = tokens // 2
    rows = enc.shape[1]
    G = S // 2 * F
    parity = lax.rem(src, 2)
    mate = src + 1 - 2 * parity
    group = (src // 2) * F + feat
    chunk = 32 if wf % 32 == 0 else 16
    chunks = wf // chunk
    pieces = 2 if wf % 32 == 0 else 1
    part = wf // pieces
    early = lax.rem(tgt, 2)
    has_in = (tgt > 0) & (src < tgt * K)
    has_out = (tgt < T - 1) & (src < (tgt + 1) * K)
    late = 1 - early
    H = S // 2
    side = src // 2

    barrier = pltpu.get_barrier_semaphore()
    plane = src * F + feat

    def greet(i):
        other = lax.rem(plane + i, S * F)
        pl.semaphore_signal(barrier, inc=1, device_id=(other // F, tgt, lax.rem(other, F)),
                            device_id_type=MESH)

    each(S * F, greet, 1)

    @pl.when(tgt > 0)
    def _():
        pl.semaphore_signal(barrier, inc=1, device_id=(src, tgt - 1, feat), device_id_type=MESH)

    @pl.when(tgt < T - 1)
    def _():
        pl.semaphore_signal(barrier, inc=1, device_id=(src, tgt + 1, feat), device_id_type=MESH)

    own_ids = ids[pl.ds(src, 1), :]
    idcol[...] = jnp.transpose(jnp.broadcast_to(own_ids, (128, FW)))

    def picked(f_index, r):
        start = pl.multiple_of(f_index * wf + r * part, 16)
        col = idcol[pl.ds(start, part), :][:, :1] - feat * raw
        one_hot = (col == lax.broadcasted_iota(jnp.int32, (part, raw), 1)).astype(
            jnp.float32).astype(jnp.bfloat16)
        some = acts[0, pl.ds(pl.multiple_of(early * half, 16), half), :]
        return lax.dot_general(one_hot, some, NT,
                               preferred_element_type=jnp.float32).astype(jnp.bfloat16)

    def remote(a, b, s, r, where):
        return pltpu.make_async_remote_copy(src_ref=a, dst_ref=b, send_sem=s, recv_sem=r,
                                            device_id=where, device_id_type=MESH)

    def chain_copy(i):
        at = pl.ds(pl.multiple_of(i * chunk, 16), chunk)
        return remote(ch_send.at[at], ch_recv.at[at], c_s.at[i], c_r.at[i],
                      (src, lax.rem(tgt + 1, T), feat))

    def chain(first, last):
        def step(i, carry):
            at = pl.ds(pl.multiple_of(i * chunk, 16), chunk)

            @pl.when(has_in)
            def _():
                chain_copy(i).wait_recv()

            total = ch_recv[at, :].astype(jnp.float32)
            for k in range(K):
                prefix[k, at, :] = total.astype(jnp.bfloat16)
                live = (tgt * K + k >= src).astype(jnp.float32)
                total = total + dec[0, k, at, :].astype(jnp.float32) * live

            @pl.when(has_out)
            def _():
                ch_send[at, :] = total.astype(jnp.bfloat16)
                chain_copy(i).start()
            return carry
        lax.fori_loop(first, last, step, 0)

    def e_at(p):
        return e_all.at[:, pl.ds(pl.multiple_of(p * rows, 16), rows), :]

    def place(h, f, par):
        return (2 * h + par) * F + f

    def e_y(j):
        return remote(enc, e_at(plane), ey_s.at[j], ey_r.at[j], (src, tgt, lax.rem(feat + j, F)))

    def e_x(i, j, source=None):
        at = e_at(place(side, lax.rem(feat - j + F, F), parity))
        return remote(enc if source is None else source, at, ex_s.at[i, j], ex_r.at[i, j],
                      (2 * lax.rem(side + i, H) + parity, tgt, feat))

    def e_x_out(i, j):
        if isinstance(j, int) and j == 0:
            return e_x(i, 0)
        return e_x(i, j, e_at(place(side, lax.rem(feat - j + F, F), parity)))

    def e_mate(i, j, par, own=False):
        at = e_at(place(lax.rem(side - i + H, H), lax.rem(feat - j + F, F), par))
        return remote(enc if own else at, at, ef_s.at[i, j], ef_r.at[i, j], (mate, tgt, feat))

    def p_copy(r, j):
        return remote(pt_send.at[r, j - 1], pt_recv.at[r, j - 1], p_s.at[r, j - 1],
                      p_r.at[r, j - 1], (src, tgt, lax.rem(feat + j, F)))

    def z_copy(r, q):
        at = w_own.at[q, pl.ds(r * part, part), :]
        return remote(at, at, z_s.at[r], z_r.at[r], (src, tgt + 1 - 2 * early, feat))

    def w_at(r, q, k, f):
        return w_all.at[q, k, pl.ds(pl.multiple_of(f * wf + r * part, 16), part), :]

    def w_copy(n, r, q, k, j):
        g = lax.rem(group + j, G)
        return remote(w_own.at[q, pl.ds(r * part, part), :], w_at(r, q, k, feat),
                      w_s.at[n, r, k, j], w_r.at[r, k, feat],
                      (2 * (g // F) + q, tgt, lax.rem(g, F)))

    def w_move(r, k, f, par, s, d):
        at = w_at(r, par, k, f)
        return remote(at, at, s.at[r, k, f], d.at[r, k, f], (mate, tgt, feat))

    def w_arrival(r, k, f):
        return w_move(r, k, f, parity, wf_s, w_r)

    def w_forward(r, k, f):
        return w_move(r, k, f, parity, wf_s, wf_r)

    def w_forward_in(r, k, f):
        return w_move(r, k, f, 1 - parity, wf_s, wf_r)

    def if_sends(q, k, j, fn):
        owner = src == tgt * K + k
        if isinstance(j, int) and j > 0:
            pl.when(owner)(fn)
        else:
            pl.when(owner & ((j > 0) | (parity != q)))(fn)

    @pl.when(jnp.logical_not(has_in))
    def _():
        ch_recv[...] = jnp.zeros_like(ch_recv)

    @pl.when(has_in & (tgt == T - 1))
    def _():
        out[...] = jnp.zeros_like(out)

    pl.semaphore_wait(barrier, S * F - 1 + (tgt > 0).astype(jnp.int32)
                      + (tgt < T - 1).astype(jnp.int32))

    @pl.when(jnp.logical_not(has_in))
    def _():
        chain(0, chunks)

    for r in range(pieces):
        for j in range(1, F):
            pt_send[r, j - 1] = picked(lax.rem(feat + j, F), r)
            p_copy(r, j).start()

    each(H, lambda i: e_x_out(i, 0).start(), 1)
    e_mate(0, 0, parity, True).start()
    local = pltpu.make_async_copy(enc, e_at(plane), l_s)
    local.start()
    for r in range(pieces):
        w_own[early, r * part:(r + 1) * part] = picked(feat, r)
    marks = [0, chunks * 3 // 10, chunks * 5 // 10, chunks * 8 // 10, chunks]

    def chain_part(n):
        @pl.when(has_in & (tgt < T - 1))
        def _():
            chain(marks[n], marks[n + 1])

    def mine(k, f):
        return (src == tgt * K + k) & (feat == f)

    def mates(k, f):
        return (mate == tgt * K + k) & (feat == f)

    def w_send(n, r, q):
        for k in range(K):
            def send(j):
                if_sends(q, k, j, lambda: w_copy(n, r, q, k, j).start())
            each(G, send)

            @pl.when(src == tgt * K + k)
            def _():
                w_all[q, k, pl.ds(pl.multiple_of(feat * wf + r * part, 16), part), :] = (
                    w_own[q, r * part:(r + 1) * part])

    def w_pass():
        for r in range(pieces):
            for k in range(K):
                for f in range(F):
                    @pl.when(jnp.logical_not(mine(k, f)))
                    def _():
                        w_arrival(r, k, f).wait_recv()

                    @pl.when(jnp.logical_not(mates(k, f)))
                    def _():
                        w_forward(r, k, f).start()

    chain_part(0)
    for r in range(pieces):
        at = slice(r * part, (r + 1) * part)
        for j in range(1, F):
            p_copy(r, j).wait_recv()
            w_own[early, at] = w_own[early, at] + pt_recv[r, j - 1]
        z_copy(r, early).start()
        w_send(0, r, early)
    each(F, lambda j: e_y(j).start(), 1)
    chain_part(1)

    def e_turn(j):
        e_y(j).wait_recv()
        each(H, lambda i: e_x_out(i, j).start(), 1)
        e_mate(0, j, parity).start()

    each(F, e_turn, 1)
    chain_part(2)
    for r in range(pieces):
        z_copy(r, late).wait_recv()
        w_send(1, r, late)
    pl.when(parity == early)(w_pass)

    def e_far(i, j):
        e_x(i, j).wait_recv()
        e_mate(i, j, parity).start()

    each(H, lambda i: each(F, lambda j: e_far(i, j)), 1)
    chain_part(3)

    each(H, lambda i: each(F, lambda j: e_mate(i, j, 1 - parity).wait_recv()))
    local.wait()
    ends = has_in & (tgt == T - 1)

    def virtual(k):
        return jnp.dot(prefix[k], e_all[k], preferred_element_type=jnp.float32)

    @pl.when(jnp.logical_not(ends))
    def _():
        for k in range(K):
            out[0, k] = virtual(k)

    pl.when(parity == late)(w_pass)

    for k in range(K):
        for f in range(F):
            @pl.when(jnp.logical_not(mine(k, f)))
            def _():
                for r in range(pieces):
                    w_forward_in(r, k, f).wait_recv()
        gram = lax.dot_general(w_own[0], w_all[0, k], NT, preferred_element_type=jnp.float32)
        gram += lax.dot_general(w_own[1], w_all[1, k], NT, preferred_element_type=jnp.float32)
        gram = gram / tokens
        out[0, k] = jnp.where(ends, gram, out[0, k] * gram)

    @pl.when(ends)
    def _():
        chain(0, chunks)
        for k in range(K):
            out[0, k] = virtual(k) * out[0, k]

    @pl.when(has_out)
    def _():
        each(chunks, lambda i: chain_copy(i).wait_send())

    for r in range(pieces):
        for j in range(1, F):
            p_copy(r, j).wait_send()
        z_copy(r, early).wait_send()
    for n, q in ((0, early), (1, late)):
        for k in range(K):
            for r in range(pieces):
                def sent(j):
                    if_sends(q, k, j, lambda: w_copy(n, r, q, k, j).wait_send())
                each(G, sent)
    each(F, lambda j: e_y(j).wait_send(), 1)
    each(H, lambda i: each(F, lambda j: e_x_out(i, j).wait_send()), 1)
    each(H, lambda i: each(F, lambda j: e_mate(i, j, parity).wait_send()))
    for k in range(K):
        for f in range(F):
            @pl.when(jnp.logical_not(mates(k, f)))
            def _():
                for r in range(pieces):
                    w_forward(r, k, f).wait_send()


def solution(mesh):
    S, T, F = mesh.shape["src"], mesh.shape["tgt"], mesh.shape["feat"]

    def per_device(activations, window_ids, decoders, encoders):
        _, tokens, raw = activations.shape
        FW = window_ids.shape[1]
        _, K, wf, D = decoders.shape
        G = S // 2 * F
        H = S // 2
        pieces = 2 if wf % 32 == 0 else 1
        bf = jnp.bfloat16
        dma = pltpu.SemaphoreType.DMA
        chunks = wf // (32 if wf % 32 == 0 else 16)
        vmem = pl.BlockSpec(memory_space=pltpu.VMEM)
        return pl.pallas_call(
            functools.partial(kernel, S, T, F),
            out_shape=pltpu.VMEM((1, K, wf, FW), jnp.float32),
            in_specs=[vmem] * 4,
            out_specs=vmem,
            scratch_shapes=[
                pltpu.VMEM((FW, 128), jnp.int32),
                pltpu.VMEM((pieces, F - 1, wf // pieces, tokens // 2), bf),
                pltpu.VMEM((pieces, F - 1, wf // pieces, tokens // 2), bf),
                pltpu.VMEM((2, wf, tokens // 2), bf),
                pltpu.VMEM((2, K, FW, tokens // 2), bf),
                pltpu.VMEM((K, D, FW), bf),
                pltpu.VMEM((wf, D), bf),
                pltpu.VMEM((wf, D), bf),
                pltpu.VMEM((K, wf, D), bf),
                dma((pieces, F - 1)), dma((pieces, F - 1)), dma((pieces,)), dma((pieces,)),
                dma((F,)), dma((F,)), dma((H, F)), dma((H, F)), dma((H, F)), dma((H, F)),
                dma((2, pieces, K, G)), dma((pieces, K, F)), dma((pieces, K, F)),
                dma((pieces, K, F)),
                dma((chunks,)), dma((chunks,)), dma(()),
            ],
            compiler_params=pltpu.CompilerParams(
                collective_id=0, has_side_effects=True, vmem_limit_bytes=56 * 2**20),
        )(activations, window_ids, decoders, encoders)

    in_specs = (
        P("src", None, "feat"),
        P(),
        P("src", "tgt", "feat", None),
        P("tgt", ("src", "feat"), None),
    )
    return jax.shard_map(
        per_device, mesh=mesh, in_specs=in_specs, out_specs=P("src", "tgt", "feat", None),
        check_vma=False,
    )
```
